512 devices in a mesh: layer: 32 (over x, z), space: 16 (over y, core).
Axes of the slice: x: 4, y: 8, z: 8, core: 2. Of those that a mesh axis runs over, the one named last changes fastest.
Arguments:
- image: bfloat16 [64, 64, 256], P(None, 'space'), may hold values from -6 to 6
- weights: bfloat16 [128, 64, 576], P('layer'), may hold values from -0.25 to 0.25
Outputs:
- states: bfloat16 [32, 64, 64, 256], P('layer', None, 'space')
The draws below stay inside these ranges and needn't reach their ends.
All inputs are finite; a program needn't handle non-finite values.
Results may differ from the reference program's by a relative error of at most 0.019.
The reference program's roundings to bfloat16 on the way count: a program that leaves them out, or rounds other values in their place, can miss the bound.
Values may be sent and summed in bfloat16 or wider, within the bound.
No kernel may reach another device: no remote copies, remote signals or barrier semaphores. Data moves between devices by JAX's collectives and lax.ppermute only.
A program may use at most 64 MiB of HBM per device.

```python
import jax
import jax.numpy as jnp
from jax import lax

C = 64
W = 256
LAYERS_DEV = 4
CYCLES = 2
H = 64
LAYERS = 128
N_LAYER = 32


def block_levels(own_key, extent, cuts, smallest, high):
    def one(dim, blocks):
        draws = jax.random.uniform(jax.random.fold_in(jax.random.fold_in(own_key, 6), dim), (blocks,), jnp.float32, smallest / len(cuts), high / len(cuts))
        return jnp.repeat(jnp.exp(draws), extent[dim] // blocks).reshape((-1,) + (1,) * (len(extent) - dim - 1))

    loudness = one(*cuts[0])
    for cut in cuts[1:]:
        loudness = loudness * one(*cut)
    return loudness


def centred(own_key, shape, deviation, reach, split=(), kind=jnp.bfloat16):
    drawn = jax.random.normal(own_key, shape, jnp.float32) * deviation
    if len(split) > 0:
        drawn = block_levels(own_key, shape, split, -0.22, 0.18) * drawn
    return jnp.clip(drawn, min=-reach, max=reach).astype(kind)


def setup_inputs(seed: int = 0) -> dict:
    arg_keys = jax.random.split(jax.random.key(seed), 3)
    return {
        "image": centred(arg_keys[0], (C, H, W), 1.0, 6.0, ((1, 16),)),
        "weights": centred(arg_keys[1], (LAYERS, C, 9 * C), (9 * C) ** -0.5, 0.25, ((0, 32),)),
    }


STEP = 0.125


def conv_same(field, kernel):
    height = field.shape[1]
    width = field.shape[2]
    padded = jnp.pad(field, ((0, 0), (1, 1), (1, 1)))
    taps = jnp.concatenate([padded[:, dy:dy + height, dx:dx + width] for dy in range(3) for dx in range(3)], 0)
    flat = taps.reshape(taps.shape[0], height * width)
    return jnp.dot(kernel, flat, preferred_element_type=jnp.float32).reshape(kernel.shape[0], height, width)


def layer_step(field, kernel):
    return (field.astype(jnp.float32) + STEP * jnp.tanh(conv_same(field, kernel))).astype(jnp.bfloat16)


def run_block(field, kernels):
    def apply(carry, kernel):
        return layer_step(carry, kernel), None
    return lax.scan(apply, field, kernels)[0]


def pooled(field):
    chans, height, width = field.shape
    return field.astype(jnp.float32).reshape(chans, height // 2, 2, width // 2, 2).mean(axis=(2, 4))


def widened(field):
    return jnp.repeat(jnp.repeat(field, 2, axis=1), 2, axis=2)


def coarse_step(state, kernel):
    return state + LAYERS_DEV * STEP * jnp.tanh(conv_same(state.astype(jnp.bfloat16), kernel))


def reference(image, weights):
    blocks = weights.reshape(N_LAYER, LAYERS_DEV, weights.shape[1], weights.shape[2])
    coarse_kernels = jnp.mean(blocks.astype(jnp.float32), axis=1).astype(jnp.bfloat16)
    start = pooled(image)
    states = jnp.broadcast_to(image, (N_LAYER,) + image.shape)
    for cycle in range(CYCLES):
        ends = lax.map(lambda pair: run_block(pair[0], pair[1]), (states, blocks))
        tau = lax.map(lambda trio: pooled(trio[0]) - coarse_step(pooled(trio[1]), trio[2]), (ends, states, coarse_kernels))

        def chain(state, pair):
            following = coarse_step(state, pair[0]) + pair[1]
            return following, following

        levels = lax.scan(chain, start, (coarse_kernels[:-1], tau[:-1]))[1]
        before = ends[:-1]
        fixed = lax.map(lambda pair: (pair[0].astype(jnp.float32) + widened(pair[1] - pooled(pair[0]))).astype(jnp.bfloat16), (before, levels))
        states = jnp.concatenate([image[None], fixed], 0)
    return states
```

```python
import functools

import jax
import jax.numpy as jnp
from jax import lax
from jax.experimental import pallas as pl
from jax.experimental.pallas import tpu as pltpu
from jax.sharding import Mesh
from jax.sharding import PartitionSpec as P


STEP = 0.125
C = 64
FU, CU = 32, 16
FL, CL = 256, 128
OWN = 16
EDGE = 11
WIDTH = 256
BLOCKS = 4
PLANES, ZS, YS = 4, 8, 8
F32, BF16 = jnp.float32, jnp.bfloat16


def unit(u, count=1):
    start = u * C
    if not isinstance(u, int):
        start = pl.multiple_of(start, C)
    return pl.ds(start, count * C)


def lane_of(shape):
    return lax.broadcasted_iota(jnp.int32, shape, 1)


def pool_matrix():
    rows = lax.broadcasted_iota(jnp.int32, (FL, CL), 0)
    return jnp.where((rows >> 1) == lane_of((FL, CL)), 0.25, 0.0).astype(BF16)


def widen_matrix():
    rows = lax.broadcasted_iota(jnp.int32, (CL, FL), 0)
    return jnp.where(rows == (lane_of((CL, FL)) >> 1), 1.0, 0.0).astype(BF16)


def fine_factor(z):
    column = (lane_of((1, FL)) & 127) + (2 * OWN * z - 2 * EDGE)
    return jnp.where((column >= 0) & (column < WIDTH), STEP, 0.0).astype(F32)


def coarse_factor(z):
    column = (lane_of((1, CL)) & 63) + (OWN * z - EDGE)
    return jnp.where((column >= 0) & (column < WIDTH // 2), BLOCKS * STEP, 0.0).astype(F32)


def dot(a, b):
    return jnp.dot(a, b, preferred_element_type=F32)


def shifted_sum(product):
    parts = []
    for at in range(0, product.shape[1], 128):
        block = product[:, at : at + 128]
        parts.append(
            pltpu.roll(block[:C], 1, 1) + block[C : 2 * C] + pltpu.roll(block[2 * C :], 127, 1)
        )
    return parts[0] if len(parts) == 1 else jnp.concatenate(parts, axis=1)


def arranged(kernel):
    return jnp.concatenate(
        [
            jnp.concatenate(
                [kernel[:, (3 * dy + dx) * C : (3 * dy + dx + 1) * C] for dy in range(3)], axis=1
            )
            for dx in range(3)
        ],
        axis=0,
    )


def fine_halo(ref):
    zero = jnp.zeros((C, 128), BF16)
    ref[unit(0), :128] = zero
    ref[unit(0), 128:] = ref[unit(FU), :128]
    ref[unit(FU + 1), :128] = ref[unit(1), 128:]
    ref[unit(FU + 1), 128:] = zero


def coarse_halo(ref, first, last):
    lane = lane_of((C, CL))
    ref[unit(0), :] = jnp.where(lane >= 64, pltpu.roll(last, 64, 1), 0.0).astype(BF16)
    ref[unit(CU + 1), :] = jnp.where(lane < 64, pltpu.roll(first, 64, 1), 0.0).astype(BF16)


def pooled_pair(first, second, matrix):
    return dot(first, matrix) + dot(second, matrix)


def corrected(first, second, level, pool, widen):
    change = level - pooled_pair(first, second, pool)
    high = change.astype(BF16)
    low = (change - high.astype(F32)).astype(BF16)
    wide = dot(high, widen) + dot(low, widen)
    return (first.astype(F32) + wide).astype(BF16), (second.astype(F32) + wide).astype(BF16)


def sweep_kernel(later, *refs):
    if later:
        sc, w_ref, img, prev, recv, level, _, _, tau_out, ends_out, xa, xb, sp, sb, wk, ck = refs
    else:
        sc, w_ref, img = refs[:3]
        tau_out, ends_out, ck_out, start_out, xa, xb, sp, sb, wk, ck = refs[-10:]
    z = sc[1]
    pool = pool_matrix()
    mf = fine_factor(z)
    mc = coarse_factor(z)

    for l in range(4):
        wk[l] = arranged(w_ref[l])
    total = w_ref[0].astype(F32) + w_ref[1].astype(F32) + w_ref[2].astype(F32) + w_ref[3].astype(F32)
    ck[...] = arranged((total * 0.25).astype(BF16))
    if not later:
        ck_out[0] = ck[...]

    def from_image():
        @pl.loop(0, FU, unroll=8)
        def _(u):
            xa[unit(u + 1), :] = img[u]

    if later:
        widen = widen_matrix()

        def from_rows(rows):
            @pl.loop(0, CU, unroll=4)
            def _(u):
                one, two = corrected(
                    rows[0, 2 * u], rows[0, 2 * u + 1], level[0, u], pool, widen
                )
                xa[unit(2 * u + 1), :] = one
                xa[unit(2 * u + 2), :] = two

        pl.when(sc[2] == 0)(lambda: from_rows(prev))
        pl.when(sc[2] == 1)(lambda: from_rows(recv))
        pl.when(sc[2] == 2)(from_image)
    else:
        from_image()
    fine_halo(xa)

    @pl.loop(0, CU, unroll=4)
    def _(u):
        s = pooled_pair(xa[unit(2 * u + 1), :], xa[unit(2 * u + 2), :], pool)
        sp[unit(u), :] = s
        sb[unit(u + 1), :] = s.astype(BF16)
        if not later:
            start_out[u] = s

    coarse_halo(sb, sp[unit(0), :], sp[unit(CU - 1), :])

    for l in range(4):
        src, dst = (xa, xb) if l % 2 == 0 else (xb, xa)
        kernel = wk[l]

        @pl.loop(0, FU, unroll=8)
        def _(u, src=src, dst=dst, kernel=kernel, l=l):
            conv = shifted_sum(dot(kernel, src[unit(u, 3), :]))
            x = src[unit(u + 1), :].astype(F32)
            new = (x + mf * jnp.tanh(conv)).astype(BF16)
            dst[unit(u + 1), :] = new
            if l == 3:
                ends_out[0, u] = new

        if l < 3:
            fine_halo(dst)

    kernel = ck[...]

    @pl.loop(0, CU, unroll=8)
    def _(u):
        ends = pooled_pair(xa[unit(2 * u + 1), :], xa[unit(2 * u + 2), :], pool)
        conv = shifted_sum(dot(kernel, sb[unit(u, 3), :]))
        tau_out[0, u] = ends - (sp[unit(u), :] + mc * jnp.tanh(conv))


def whole(shape, dtype=None):
    return pl.BlockSpec(shape, lambda i, s: (0,) * len(shape))


def at_own(shape):
    return pl.BlockSpec((1,) + shape, lambda i, s: (s[0],) + (0,) * len(shape))


TAU = (BLOCKS, CU, C, CL)
ENDS = (BLOCKS, FU, C, FL)
KER = (BLOCKS, 3 * C, 3 * C)
VMEM_LIMIT = 56 * 1024 * 1024

SWEEP_SCRATCH = [
    pltpu.VMEM(((FU + 2) * C, FL), BF16),
    pltpu.VMEM(((FU + 2) * C, FL), BF16),
    pltpu.VMEM((CU * C, CL), F32),
    pltpu.VMEM(((CU + 2) * C, CL), BF16),
    pltpu.VMEM((4, 3 * C, 3 * C), BF16),
    pltpu.VMEM((3 * C, 3 * C), BF16),
]
SWEEP_COST = pl.CostEstimate(flops=2 * 4 * 192 * 192 * FU * FL, bytes_accessed=5 << 20, transcendentals=4 * C * FU * FL)


def first_sweep(scalars, weights, image, earlier):
    shapes = [
        jax.ShapeDtypeStruct(TAU, F32),
        jax.ShapeDtypeStruct(ENDS, BF16),
        jax.ShapeDtypeStruct(KER, BF16),
        jax.ShapeDtypeStruct((CU, C, CL), F32),
    ]
    extra = list(earlier) if earlier else []
    return pl.pallas_call(
        functools.partial(sweep_kernel, False),
        out_shape=shapes,
        grid_spec=pltpu.PrefetchScalarGridSpec(
            num_scalar_prefetch=1,
            grid=(1,),
            in_specs=[whole((4, C, 9 * C)), whole((FU, C, FL))]
            + [pl.BlockSpec(memory_space=pl.ANY)] * len(extra),
            out_specs=[at_own(TAU[1:]), at_own(ENDS[1:]), at_own(KER[1:]), whole((CU, C, CL))],
            scratch_shapes=SWEEP_SCRATCH,
        ),
        input_output_aliases={3 + i: i for i in range(len(extra))},
        compiler_params=pltpu.CompilerParams(vmem_limit_bytes=VMEM_LIMIT),
        cost_estimate=SWEEP_COST,
    )(scalars, weights, image, *extra)


def later_sweep(scalars, weights, image, ends, received, levels, tau_buffer, ends_buffer):
    def before(i, s):
        return (jnp.maximum(s[0] - 1, 0), 0, 0, 0)

    return pl.pallas_call(
        functools.partial(sweep_kernel, True),
        out_shape=[jax.ShapeDtypeStruct(TAU, F32), jax.ShapeDtypeStruct(ENDS, BF16)],
        grid_spec=pltpu.PrefetchScalarGridSpec(
            num_scalar_prefetch=1,
            grid=(1,),
            in_specs=[
                whole((4, C, 9 * C)),
                whole((FU, C, FL)),
                pl.BlockSpec((1,) + ENDS[1:], before),
                whole((1,) + ENDS[1:]),
                at_own(TAU[1:]),
                pl.BlockSpec(memory_space=pl.ANY),
                pl.BlockSpec(memory_space=pl.ANY),
            ],
            out_specs=[at_own(TAU[1:]), at_own(ENDS[1:])],
            scratch_shapes=SWEEP_SCRATCH,
        ),
        input_output_aliases={6: 0, 7: 1},
        compiler_params=pltpu.CompilerParams(vmem_limit_bytes=VMEM_LIMIT),
        cost_estimate=SWEEP_COST,
    )(scalars, weights, image, ends, received, levels, tau_buffer, ends_buffer)


def chain_kernel(sc, below, same, above, start, tau_own, tau_other, ck_own, ck_other, levels, pack, lf, la, lb, ks):
    z, c, fresh = sc[0], sc[1], sc[2]
    mc = coarse_factor(z)
    lane = lane_of((C, CL)) & 63

    def order(low, high):
        ks[:BLOCKS] = low[...]
        ks[BLOCKS:] = high[...]

    pl.when(c == 0)(lambda: order(ck_own, ck_other))
    pl.when(c == 1)(lambda: order(ck_other, ck_own))

    @pl.when(fresh == 1)
    def _():
        @pl.loop(0, CU, unroll=4)
        def _(u):
            lf[unit(u), :] = start[u]

    @pl.when(fresh == 0)
    def _():
        for u in range(CU):
            a, i = u // 4, u % 4

            def placed(ref, by):
                return pltpu.roll(ref[a].astype(F32), (by - 16 * i) % 128, 1)

            value = jnp.where(lane < EDGE, placed(below, EDGE - 16), placed(same, EDGE))
            value = jnp.where(lane < EDGE + OWN, value, placed(above, EDGE + 16))
            lf[unit(u), :] = jnp.where((lane >= 2) & (lane < 36), value, 0.0)

    @pl.loop(0, CU, unroll=4)
    def _(u):
        la[unit(u + 1), :] = lf[unit(u), :].astype(BF16)

    coarse_halo(la, lf[unit(0), :], lf[unit(CU - 1), :])

    def step(j, src, dst):
        at = j & (BLOCKS - 1)
        own = (j >> 2) == c

        @pl.when(own)
        def _():
            @pl.loop(0, CU, unroll=4)
            def _(u):
                levels[at, u] = lf[unit(u), :]

        kernel = ks[j]

        @pl.loop(0, CU, unroll=8)
        def _(u):
            conv = shifted_sum(dot(kernel, src[unit(u, 3), :]))
            tau = jnp.where(own, tau_own[at, u], tau_other[at, u])
            new = lf[unit(u), :] + mc * jnp.tanh(conv) + tau
            lf[unit(u), :] = new
            dst[unit(u + 1), :] = new.astype(BF16)

        coarse_halo(dst, lf[unit(0), :], lf[unit(CU - 1), :])

    @pl.loop(0, BLOCKS)
    def _(t):
        step(2 * t, la, lb)
        step(2 * t + 1, lb, la)

    for a in range(4):
        total = jnp.zeros((C, CL), F32)
        for i in range(4):
            moved = pltpu.roll(lf[unit(4 * a + i), :], (16 * i - EDGE) % 128, 1)
            total = jnp.where((lane >= 16 * i) & (lane < 16 * i + 16), moved, total)
        pack[a] = total.astype(pack.dtype)


PACK = (4, C, CL)


def chain(scalars, packs, start, tau_own, tau_other, ck_own, ck_other):
    vmem = pl.BlockSpec(memory_space=pltpu.VMEM)
    return pl.pallas_call(
        chain_kernel,
        out_shape=[jax.ShapeDtypeStruct(TAU, F32), jax.ShapeDtypeStruct(PACK, BF16)],
        in_specs=[pl.BlockSpec(memory_space=pltpu.SMEM)] + [vmem] * 8,
        out_specs=[vmem, vmem],
        scratch_shapes=[
            pltpu.VMEM((CU * C, CL), F32),
            pltpu.VMEM(((CU + 2) * C, CL), BF16),
            pltpu.VMEM(((CU + 2) * C, CL), BF16),
            pltpu.VMEM((2 * BLOCKS, 3 * C, 3 * C), BF16),
        ],
        compiler_params=pltpu.CompilerParams(vmem_limit_bytes=VMEM_LIMIT),
        cost_estimate=pl.CostEstimate(flops=2 * 8 * 192 * 192 * CU * CL, bytes_accessed=6 << 20, transcendentals=8 * CU * C * CL),
    )(scalars, *packs, start, tau_own, tau_other, ck_own, ck_other)


def final_kernel(sc, img, ends, recv, level, out):
    y, fresh = sc[0], sc[1]
    pool, widen = pool_matrix(), widen_matrix()
    lane = lane_of((C, 128))
    top = (y & 3) * 8
    for j in range(BLOCKS):
        for k in range(2):
            packed = jnp.zeros((C, 128), F32)
            for pair in range(2):
                u = top + 4 * k + 2 * pair
                one, two = (recv[0, u], recv[0, u + 1]) if j == 0 else (ends[j - 1, u], ends[j - 1, u + 1])
                rows = corrected(one, two, level[j, u // 2], pool, widen)
                for r in range(2):
                    row = rows[r].astype(F32)
                    if j == 0:
                        row = jnp.where(fresh == 1, img[u + r].astype(F32), row)
                    half = jnp.where(y >= 4, row[:, 128:], row[:, :128])
                    i = 2 * pair + r
                    moved = pltpu.roll(half, (32 * i - 2 * EDGE) % 128, 1)
                    packed = jnp.where((lane >= 32 * i) & (lane < 32 * i + 32), moved, packed)
            out[2 * j + k] = packed.astype(BF16)


def final(scalars, image, ends, received, levels):
    vmem = pl.BlockSpec(memory_space=pltpu.VMEM)
    return pl.pallas_call(
        final_kernel,
        out_shape=jax.ShapeDtypeStruct((2 * BLOCKS, C, 128), BF16),
        in_specs=[pl.BlockSpec(memory_space=pltpu.SMEM)] + [vmem] * 4,
        out_specs=vmem,
        compiler_params=pltpu.CompilerParams(vmem_limit_bytes=VMEM_LIMIT),
    )(scalars, image, ends, received, levels)


def kernel_sources(i):
    pairs = []
    for z in range(ZS):
        for c in range(2):
            source = 4 * c + (z + i) % 4
            pairs.append((source * 2 + z // 4, z * 2 + c))
    return pairs


def per_device(image, weights):
    x, z, y, c = (lax.axis_index(name) for name in ("x", "z", "y", "c"))
    turn = z % 4

    fetched = [lax.ppermute(weights, ("z", "c"), kernel_sources(i)) for i in range(4)]
    slots = [(turn + i) % 4 for i in range(4)]
    wide = jnp.pad(image, ((0, 0), (0, 0), (2 * EDGE, 128)))
    piece = lax.dynamic_slice_in_dim(wide, 2 * OWN * z, 128, axis=2).transpose(1, 0, 2)
    rows = lax.all_gather(piece, ("y", "c"), tiled=True)
    tile = rows.reshape(2, FU, C, 128).transpose(1, 2, 0, 3).reshape(FU, C, FL)

    def scalars(*values):
        return jnp.stack([jnp.asarray(v, jnp.int32) for v in values])

    def swap(a):
        return lax.ppermute(a, "c", [(0, 1), (1, 0)])

    def hand_over(ends):
        pairs = []
        for p in range(PLANES):
            pairs.append((2 * p, 2 * p + 1))
            if p + 1 < PLANES:
                pairs.append((2 * p + 1, 2 * p + 2))
        return lax.ppermute(ends[BLOCKS - 1 :], ("x", "c"), pairs)

    def upward(pack):
        got = []
        for shift in (1, 0, -1):
            pairs = [
                (p * ZS + q, (p + 1) * ZS + q + shift)
                for p in range(PLANES - 1)
                for q in range(ZS)
                if 0 <= q + shift < ZS
            ]
            got.append(lax.ppermute(pack, ("x", "z"), pairs))
        return got

    fresh = (x == 0).astype(jnp.int32)

    def all_levels(start, tau, kernels, kernels_other):
        other = swap(tau)
        packs = [jnp.zeros(PACK, BF16)] * 3
        for phase in range(PLANES):
            levels, pack = chain(scalars(z, c, fresh), packs, start, tau, other, kernels, kernels_other)
            if phase + 1 < PLANES:
                packs = upward(pack)
        return levels

    done = None
    for i in range(4):
        done = first_sweep(scalars(slots[i], z), fetched[i], tile, done and done[:3])
        if i == 0:
            start = done[3]
    tau, ends, kernels, _ = done
    received = hand_over(ends)
    kernels_other = swap(kernels)
    levels = all_levels(start, tau, kernels, kernels_other)

    ends_later = jnp.zeros(ENDS, BF16)
    tau_later = jnp.zeros(TAU, F32)
    for i in range(4):
        first = slots[i] == 0
        source = jnp.where(first, jnp.where((c == 0) & (x == 0), 2, 1), 0)
        tau_later, ends_later = later_sweep(
            scalars(slots[i], z, source), fetched[i], tile, ends, received, levels, tau_later, ends_later
        )
    received = hand_over(ends_later)
    levels = all_levels(start, tau_later, kernels, kernels_other)

    parts = final(scalars(y, (c == 0) & (x == 0)), tile, ends_later, received, levels)
    sent = jnp.concatenate([parts, parts], 0)
    got = lax.all_to_all(sent, ("z", "c"), 0, 0, tiled=True).reshape(ZS, 2, C, 4, 2 * OWN)
    mine = lax.dynamic_index_in_dim(got, z // 4, 1, keepdims=False)
    return mine.transpose(1, 2, 0, 3).reshape(1, C, 4, WIDTH)


def solution(mesh):
    split = Mesh(mesh.devices.reshape(PLANES, ZS, YS, 2), ("x", "z", "y", "c"))
    return jax.shard_map(
        per_device,
        mesh=split,
        in_specs=(P(None, ("y", "c"), None), P(("x", "z"), None, None)),
        out_specs=P(("x", "z"), None, ("y", "c"), None),
        check_vma=False,
    )
```

```python
import functools

import jax
import jax.numpy as jnp
from jax import lax
from jax.experimental import pallas as pl
from jax.experimental.pallas import tpu as pltpu
from jax.sharding import Mesh
from jax.sharding import PartitionSpec as P


STEP = 0.125
C = 64
FU, CU = 22, 11
HEIGHT = 64
FP, CP = 80, 40
FL, CL = 256, 128
OWN = 16
EDGE = 11
WIDTH = 256
BLOCKS = 4
PLANES, ZS, YS = 4, 8, 8
F32, BF16 = jnp.float32, jnp.bfloat16


def unit(u, count=1):
    start = u * C
    if not isinstance(u, int):
        start = pl.multiple_of(start, C)
    return pl.ds(start, count * C)


def lane_of(shape):
    return lax.broadcasted_iota(jnp.int32, shape, 1)


def pool_matrix():
    rows = lax.broadcasted_iota(jnp.int32, (FL, CL), 0)
    return jnp.where((rows >> 1) == lane_of((FL, CL)), 0.25, 0.0).astype(BF16)


def widen_matrix():
    rows = lax.broadcasted_iota(jnp.int32, (CL, FL), 0)
    return jnp.where(rows == (lane_of((CL, FL)) >> 1), 1.0, 0.0).astype(BF16)


def part_of(lane, pitch):
    return (lane >= pitch).astype(jnp.int32) + (lane >= 2 * pitch).astype(jnp.int32)


def within(lane, pitch):
    return lane - pitch * part_of(lane, pitch)


def factors(z, lanes, pitch, edge, own, width, value):
    lane = lane_of((1, lanes))
    column = within(lane, pitch) + (own * z - edge)
    inside = (column >= 0) & (column < width) & (lane < 3 * pitch)
    full = jnp.where(inside, value, 0.0).astype(F32)
    return full, jnp.where(lane < 2 * pitch, full, 0.0)


def fine_factors(z):
    return factors(z, FL, FP, 2 * EDGE, 2 * OWN, WIDTH, STEP)


def coarse_factors(z):
    return factors(z, CL, CP, EDGE, OWN, WIDTH // 2, BLOCKS * STEP)


def dot(a, b):
    return jnp.dot(a, b, preferred_element_type=F32)


def shifted_sum(product):
    lanes = product.shape[1]
    return pltpu.roll(product[:C], 1, 1) + product[C : 2 * C] + pltpu.roll(product[2 * C :], lanes - 1, 1)


def arranged(kernel):
    return jnp.concatenate(
        [
            jnp.concatenate(
                [kernel[:, (3 * dy + dx) * C : (3 * dy + dx + 1) * C] for dy in range(3)], axis=1
            )
            for dx in range(3)
        ],
        axis=0,
    )


def around(first, last, pitch):
    lanes = first.shape[1]
    lane = lane_of(first.shape)
    front = jnp.where((lane >= pitch) & (lane < 3 * pitch), pltpu.roll(last, pitch, 1), 0.0)
    behind = jnp.where(lane < 2 * pitch, pltpu.roll(first, lanes - pitch, 1), 0.0)
    return front.astype(BF16), behind.astype(BF16)


def fine_halo(ref):
    front, behind = around(ref[unit(1), :].astype(F32), ref[unit(FU), :].astype(F32), FP)
    ref[unit(0), :] = front
    ref[unit(FU + 1), :] = behind


def coarse_halo(ref, first, last):
    front, behind = around(first, last, CP)
    ref[unit(0), :] = front
    ref[unit(CU + 1), :] = behind


CHUNK = 4


def pooled_rows(rows, matrix):
    halves = dot(rows, matrix)
    return [
        halves[2 * i * C : (2 * i + 1) * C] + halves[(2 * i + 1) * C : (2 * i + 2) * C]
        for i in range(rows.shape[0] // (2 * C))
    ]


def corrected(first, second, level, pooled, widen):
    change = level - pooled
    high = change.astype(BF16)
    low = (change - high.astype(F32)).astype(BF16)
    wide = dot(high, widen) + dot(low, widen)
    return (first.astype(F32) + wide).astype(BF16), (second.astype(F32) + wide).astype(BF16)


def states_from_rows(xa, rows, level, pool, widen):
    for u in range(0, CU, CHUNK):
        count = min(CHUNK, CU - u)
        block = rows[0, 2 * u : 2 * u + 2 * count].reshape(2 * count * C, FL)
        for i, pooled in enumerate(pooled_rows(block, pool)):
            one, two = corrected(
                rows[0, 2 * (u + i)], rows[0, 2 * (u + i) + 1], level[0, u + i], pooled, widen
            )
            xa[unit(2 * (u + i) + 1), :] = one
            xa[unit(2 * (u + i) + 2), :] = two


def states_from_tile(xa, tile):
    for u in range(FU):
        xa[unit(u + 1), :] = tile[u]


def pool_states(xa, sp, sb, pool):
    for u in range(0, CU, CHUNK):
        count = min(CHUNK, CU - u)
        for i, s in enumerate(pooled_rows(xa[unit(2 * u + 1, 2 * count), :], pool)):
            sp[u + i] = s
            sb[unit(u + i + 1), :] = s.astype(BF16)
    coarse_halo(sb, sp[0], sp[CU - 1])


def run_layers(wk, xa, xb, mf):
    def layer(l, src, dst):
        kernel = wk[0, l]
        for u in range(FU):
            conv = shifted_sum(dot(kernel, src[unit(u, 3), :]))
            x = src[unit(u + 1), :].astype(F32)
            dst[unit(u + 1), :] = (x + mf[u >= FU - 2] * jnp.tanh(conv)).astype(BF16)
        fine_halo(dst)

    @pl.loop(0, 2)
    def _(t):
        layer(2 * t, xa, xb)
        layer(2 * t + 1, xb, xa)


def write_tau(ck, xa, sp, sb, tau_out, pool, mc):
    kernel = ck[0]
    for u in range(0, CU, CHUNK):
        count = min(CHUNK, CU - u)
        for i, ends in enumerate(pooled_rows(xa[unit(2 * u + 1, 2 * count), :], pool)):
            conv = shifted_sum(dot(kernel, sb[unit(u + i, 3), :]))
            tau_out[0, u + i] = (ends - (sp[u + i] + mc[u + i == CU - 1] * jnp.tanh(conv))).astype(BF16)


def first_kernel(sc, w0, w1, w2, w3, source, tau, ends, wk, ck, last, tile, sp, xa, xb, sb, sem):
    step = pl.program_id(0)
    z = sc[1]
    block = (z + step) & (BLOCKS - 1)
    pool = pool_matrix()

    def take(w):
        for l in range(4):
            wk[0, l] = arranged(w[l])
        total = w[0].astype(F32) + w[1].astype(F32) + w[2].astype(F32) + w[3].astype(F32)
        ck[0] = arranged((total * 0.25).astype(BF16))

    for i, w in enumerate((w0, w1, w2, w3)):
        pl.when(step == i)(functools.partial(take, w))

    @pl.when(step == 0)
    def _():
        zero = jnp.zeros((C, FP), BF16)

        def piece(row):
            if row >= HEIGHT:
                return zero
            strip, i = row // 4, row % 4
            return source[strip, :, i * FP : (i + 1) * FP]

        for u in range(FU):
            parts = [piece(u), piece(FU + u), piece(2 * FU + u), zero[:, : FL - 3 * FP]]
            tile[u] = jnp.concatenate(parts, axis=1)

    states_from_tile(xa, tile)
    fine_halo(xa)
    pl.when(step == 0)(lambda: pool_states(xa, sp, sb, pool))
    run_layers(wk, xa, xb, fine_factors(z))

    def to_last():
        return pltpu.make_async_copy(xa.at[pl.ds(C, FU * C), :], last, sem)

    pl.when(block == BLOCKS - 1)(lambda: to_last().start())
    for u in range(FU):
        ends[0, u] = xa[unit(u + 1), :]
    write_tau(ck, xa, sp, sb, tau, pool, coarse_factors(z))
    pl.when(block == BLOCKS - 1)(lambda: to_last().wait())


def later_kernel(sc, wk, ck, before, level, tau, edge, edge_other, xa, xb, sp, sb):
    z, y, c = sc[1], sc[2], sc[3]
    pool = pool_matrix()
    states_from_rows(xa, before, level, pool, widen_matrix())
    fine_halo(xa)
    pool_states(xa, sp, sb, pool)
    run_layers(wk, xa, xb, fine_factors(z))
    for out, k in ((edge, c), (edge_other, 1 - c)):
        for r in range(4):
            row = 8 * y + 4 * k + r
            out[0, r] = xa[unit(row - FU * part_of(row, FU) + 1), :]
    write_tau(ck, xa, sp, sb, tau, pool, coarse_factors(z))


def whole(shape):
    return pl.BlockSpec(shape, lambda i, s: (0,) * len(shape))


def at_step(shape):
    return pl.BlockSpec((1,) + shape, lambda i, s: (i,) + (0,) * len(shape))


def at_slot(shape, by=0):
    return pl.BlockSpec((1,) + shape, lambda i, s: (((s[1] + i) & (BLOCKS - 1)) + by,) + (0,) * len(shape))


ANY = pl.BlockSpec(memory_space=pl.ANY)
ROWS_AT = 16
TAU = (BLOCKS, CU, C, CL)
ENDS = (BLOCKS + 1, FU, C, FL)
EDGES = (BLOCKS, 4, C, FL)
ROWS = (2 * BLOCKS, 2, C, CL)
TILE = (FU, C, FL)
START = (CU, C, CL)
KERS = (BLOCKS, 4, 3 * C, 3 * C)
KER = (BLOCKS, 3 * C, 3 * C)
LAST = (FU * C, FL)
VMEM_LIMIT = 56 * 1024 * 1024
STATES = [
    pltpu.VMEM(((FU + 2) * C, FL), BF16),
    pltpu.VMEM(((FU + 2) * C, FL), BF16),
]
POOLED = [pltpu.VMEM(((CU + 2) * C, CL), BF16)]


def sweep_cost(count):
    return pl.CostEstimate(
        flops=2 * count * 4 * 192 * 192 * FU * FL,
        bytes_accessed=count * (4 << 20),
        transcendentals=count * 4 * C * FU * FL,
    )


def first_sweeps(place, weights, source):
    return pl.pallas_call(
        first_kernel,
        out_shape=[
            jax.ShapeDtypeStruct(TAU, BF16),
            jax.ShapeDtypeStruct(ENDS, BF16),
            jax.ShapeDtypeStruct(KERS, BF16),
            jax.ShapeDtypeStruct(KER, BF16),
            jax.ShapeDtypeStruct(LAST, BF16),
            jax.ShapeDtypeStruct(TILE, BF16),
            jax.ShapeDtypeStruct(START, F32),
        ],
        grid_spec=pltpu.PrefetchScalarGridSpec(
            num_scalar_prefetch=1,
            grid=(BLOCKS,),
            in_specs=[whole((4, C, 9 * C))] * 4 + [whole((ROWS_AT, C, 4 * FP))],
            out_specs=[
                at_slot(TAU[1:]),
                at_slot(ENDS[1:], 1),
                at_slot(KERS[1:]),
                at_slot(KER[1:]),
                ANY,
                whole(TILE),
                whole(START),
            ],
            scratch_shapes=STATES + POOLED + [pltpu.SemaphoreType.DMA],
        ),
        compiler_params=pltpu.CompilerParams(vmem_limit_bytes=VMEM_LIMIT),
        cost_estimate=sweep_cost(BLOCKS),
    )(place, *weights, source)


def later_sweeps(place, wk, ck, before, levels):
    return pl.pallas_call(
        later_kernel,
        out_shape=[
            jax.ShapeDtypeStruct(TAU, BF16),
            jax.ShapeDtypeStruct(EDGES, BF16),
            jax.ShapeDtypeStruct(EDGES, BF16),
        ],
        grid_spec=pltpu.PrefetchScalarGridSpec(
            num_scalar_prefetch=1,
            grid=(BLOCKS,),
            in_specs=[at_step(KERS[1:]), at_step(KER[1:]), at_step(ENDS[1:]), at_step(TAU[1:])],
            out_specs=[at_step(TAU[1:]), at_step(EDGES[1:]), at_step(EDGES[1:])],
            scratch_shapes=STATES + [pltpu.VMEM(START, F32)] + POOLED,
        ),
        compiler_params=pltpu.CompilerParams(vmem_limit_bytes=VMEM_LIMIT),
        cost_estimate=sweep_cost(BLOCKS),
    )(place, wk, ck, before, levels)


def chain_kernel(plane, ending, sc, below, same, above, start, tau_own, tau_other, ck_own, ck_other, *refs):
    opening = plane == 0
    if opening:
        levels, pack, lf, la, lb, ks, ts, lv, lr, pk, sems, out_sems = refs
    else:
        _, levels, pack, lf, la, lb, ks, ts, lv, lr, pk, sems, out_sems = refs
    x, z, y, c = sc[0], sc[1], sc[2], sc[3]

    def half(h):
        return slice(128 * h, 128 * h + 128)

    def fetches(j, tau, kernel):
        at = j & (BLOCKS - 1)
        return (
            pltpu.make_async_copy(kernel.at[at], ks.at[j], sems.at[2 * BLOCKS + j]),
            pltpu.make_async_copy(tau.at[at], ts.at[j], sems.at[j]),
        )

    def begin(j):
        def start(tau, kernel):
            for copy in fetches(j, tau, kernel):
                copy.start()

        pl.when((j >> 2) == c)(lambda: start(tau_own, ck_own))
        pl.when((j >> 2) != c)(lambda: start(tau_other, ck_other))

    def level_copy(slot):
        return pltpu.make_async_copy(lv.at[slot], levels.at[slot], out_sems.at[slot])

    @pl.when(x == plane)
    def _():
        if opening:
            begin_at = [pltpu.make_async_copy(start, lv.at[BLOCKS], sems.at[4 * BLOCKS])]
        else:
            begin_at = [
                pltpu.make_async_copy(ref, pk.at[i], sems.at[4 * BLOCKS + i])
                for i, ref in enumerate((below, same, above))
            ]
        for copy in begin_at:
            copy.start()
        for j in range(AHEAD):
            begin(j)
        mc = coarse_factors(z)
        lane = within(lane_of((C, CL)), CP)
        inside = lane_of((C, CL)) < 3 * CP
        for copy in begin_at:
            copy.wait()

        def halo_of(ref):
            front, behind = around(lf[unit(0), half(0)], lf[unit(4), half(1)], CP)
            ref[unit(0), half(0)] = front
            ref[unit(0), half(1)] = lf[unit(5), half(0)].astype(BF16)
            ref[unit(7), half(0)] = lf[unit(0), half(1)].astype(BF16)
            ref[unit(6), half(1)] = behind

        def put(u, h, value):
            lf[unit(u), half(h)] = value
            la[unit(u + 1), half(h)] = value.astype(BF16)

        if opening:
            lf[unit(HU - 1), half(1)] = jnp.zeros((C, CL), F32)

            @pl.loop(0, HU)
            def _(u):
                put(u, 0, lv[BLOCKS, u])

            @pl.loop(0, CU - HU)
            def _(u):
                put(u, 1, lv[BLOCKS, HU + u])

        else:

            @pl.loop(0, HU // 2)
            def _(a):
                for h in range(2):
                    pieces = [pk[n, a + h * (HU // 2)].astype(F32) for n in range(3)]
                    for i in range(2):

                        def placed(n, by):
                            return pltpu.roll(pieces[n], (by - 16 * i) % 128, 1)

                        value = jnp.where(lane < EDGE, placed(0, EDGE - 16), placed(1, EDGE))
                        value = jnp.where(lane < EDGE + OWN, value, placed(2, EDGE + 16))
                        put(2 * a + i, h, jnp.where((lane >= 2) & (lane < 36) & inside, value, 0.0))

        halo_of(la)

        def step(j, src, dst):
            own = (j >> 2) == c
            slot = jnp.where(own, j & (BLOCKS - 1), BLOCKS)
            pl.when(j + AHEAD < 2 * BLOCKS)(lambda: begin(j + AHEAD))
            for copy in fetches(j, tau_own, ck_own):
                copy.wait()
            kernel = ks[j]
            if ending:
                for r in range(2):
                    row = 4 * y + 2 * c + r
                    u = row - CU * part_of(row, CU)
                    h = (u >= HU).astype(jnp.int32)
                    rows = lf[unit(u - HU * h), :]
                    lr[j, r] = jnp.where(h == 1, rows[:, half(1)], rows[:, half(0)])
            for u in range(HU):
                product = dot(kernel, src[unit(u, 3), :])
                for h in range(2):
                    if u + HU * h >= CU:
                        continue
                    conv = shifted_sum(product[:, half(h)])
                    old = lf[unit(u), half(h)]
                    if not ending:
                        lv[slot, u + HU * h] = old
                    new = old + mc[u + HU * h == CU - 1] * jnp.tanh(conv) + ts[j, u + HU * h].astype(F32)
                    lf[unit(u), half(h)] = new
                    dst[unit(u + 1), half(h)] = new.astype(BF16)
            halo_of(dst)
            if not ending:
                pl.when(own)(lambda: level_copy(j & (BLOCKS - 1)).start())

        @pl.loop(0, BLOCKS)
        def _(t):
            step(2 * t, la, lb)
            step(2 * t + 1, lb, la)

        @pl.loop(0, HU // 2)
        def _(a):
            for h in range(2):
                total = jnp.zeros((C, CL), F32)
                for i in range(2):
                    moved = pltpu.roll(lf[unit(2 * a + i), half(h)], (16 * i - EDGE) % 128, 1)
                    total = jnp.where((lane >= 16 * i) & (lane < 16 * i + 16), moved, total)
                pk[0, a + h * (HU // 2)] = total.astype(BF16)

        out = pltpu.make_async_copy(pk.at[0], pack, sems.at[4 * BLOCKS])
        out.start()
        if ending:
            rows_out = pltpu.make_async_copy(lr, levels, out_sems.at[0])
            rows_out.start()
            rows_out.wait()
        else:
            for slot in range(BLOCKS):
                level_copy(slot).wait()
        out.wait()


PACK = (6, C, CL)
HU = 6
AHEAD = 3


def chain(plane, ending, place, packs, start, tau_own, tau_other, ck_own, ck_other, held=None):
    operands = [*packs, start, tau_own, tau_other, ck_own, ck_other] + ([] if plane == 0 else [held])
    return pl.pallas_call(
        functools.partial(chain_kernel, plane, ending),
        out_shape=[jax.ShapeDtypeStruct(ROWS if ending else TAU, F32), jax.ShapeDtypeStruct(PACK, BF16)],
        in_specs=[pl.BlockSpec(memory_space=pltpu.SMEM)] + [ANY] * len(operands),
        out_specs=[ANY, ANY],
        scratch_shapes=[
            pltpu.VMEM((HU * C, FL), F32),
            pltpu.VMEM(((HU + 2) * C, FL), BF16),
            pltpu.VMEM(((HU + 2) * C, FL), BF16),
            pltpu.VMEM((2 * BLOCKS, 3 * C, 3 * C), BF16),
            pltpu.VMEM((2 * BLOCKS, CU, C, CL), BF16),
            pltpu.VMEM((BLOCKS + 1, CU, C, CL), F32),
            pltpu.VMEM(ROWS, F32),
            pltpu.VMEM((3,) + PACK, BF16),
            pltpu.SemaphoreType.DMA((4 * BLOCKS + 3,)),
            pltpu.SemaphoreType.DMA((BLOCKS,)),
        ],
        input_output_aliases={} if plane == 0 else {9: 0},
        compiler_params=pltpu.CompilerParams(vmem_limit_bytes=VMEM_LIMIT),
        cost_estimate=pl.CostEstimate(
            flops=2 * 8 * 192 * 192 * CU * CL, bytes_accessed=6 << 20, transcendentals=8 * CU * C * CL
        ),
    )(place, *operands)


def final_kernel(sc, tile, edge, edge_swapped, recv, level, out):
    fresh, y, c = sc[0] == 0, sc[2], sc[3]
    pool, widen = pool_matrix(), widen_matrix()
    lane = lane_of((C, 128))

    def choose(here, a, b):
        return jnp.where(here, a.astype(F32), b.astype(F32)).astype(BF16)

    pairs = [4 * y + 2 * c + pair for pair in range(2)]
    parts = [part_of(pair, CU) for pair in pairs]
    firsts = [2 * (pair - CU * part) for pair, part in zip(pairs, parts)]
    for j in range(2 * BLOCKS):
        packed = jnp.zeros((C, 128), F32)
        for pair in range(2):
            first = firsts[pair]
            if j == 0:
                rows = [
                    choose(fresh, tile[first + r], recv[0, 2 * pair + r]) for r in range(2)
                ]
            else:
                h, i = (j - 1) // BLOCKS, (j - 1) % BLOCKS
                rows = [
                    choose(c == h, edge[i, 2 * pair + r], edge_swapped[i, 2 * pair + r]) for r in range(2)
                ]
            pooled = dot(rows[0], pool) + dot(rows[1], pool)
            if j == 0:
                goal = jnp.where(fresh, pooled, level[0, pair])
            else:
                goal = level[j, pair]
            for r, row in enumerate(corrected(rows[0], rows[1], goal, pooled, widen)):
                row = row.astype(F32)
                i = 2 * pair + r
                moved = pltpu.roll(row, (FL - 2 * EDGE + 32 * i - FP * parts[pair]) & (FL - 1), 1)[:, :128]
                packed = jnp.where((lane >= 32 * i) & (lane < 32 * i + 32), moved, packed)
        out[j] = packed.astype(BF16)


def final(place, tile, edge, edge_swapped, received, rows):
    return pl.pallas_call(
        final_kernel,
        out_shape=jax.ShapeDtypeStruct((2 * BLOCKS, C, 128), BF16),
        grid_spec=pltpu.PrefetchScalarGridSpec(
            num_scalar_prefetch=1,
            grid=(1,),
            in_specs=[
                whole(TILE),
                whole(EDGES),
                whole(EDGES),
                whole((1,) + EDGES[1:]),
                whole(ROWS),
            ],
            out_specs=whole((2 * BLOCKS, C, 128)),
        ),
        compiler_params=pltpu.CompilerParams(vmem_limit_bytes=VMEM_LIMIT),
    )(place, tile, edge, edge_swapped, received, rows)


def kernel_sources(i):
    pairs = []
    for z in range(ZS):
        for c in range(2):
            source = 4 * c + (z + i) % 4
            pairs.append((source * 2 + z // 4, z * 2 + c))
    return pairs


def per_device(image, weights):
    x, z, y, c = (lax.axis_index(name) for name in ("x", "z", "y", "c"))
    place = jnp.stack([x, z, y, c]).astype(jnp.int32)

    def swap(a):
        return lax.ppermute(a, "c", [(0, 1), (1, 0)])

    def hand_over(last):
        pairs = []
        for p in range(PLANES):
            pairs.append((2 * p, 2 * p + 1))
            if p + 1 < PLANES:
                pairs.append((2 * p + 1, 2 * p + 2))
        return lax.ppermute(last, ("x", "c"), pairs)

    def upward(pack, p):
        got = []
        for shift in (1, 0, -1):
            pairs = [
                (p * ZS + q, (p + 1) * ZS + q + shift) for q in range(ZS) if 0 <= q + shift < ZS
            ]
            got.append(lax.ppermute(pack, ("x", "z"), pairs))
        return got

    fetched = [lax.ppermute(weights, ("z", "c"), kernel_sources(i)) for i in range(BLOCKS)]
    wide = jnp.pad(image, ((0, 0), (0, 0), (2 * EDGE, 128)))
    piece = lax.dynamic_slice_in_dim(wide, 2 * OWN * z, FP, axis=2).reshape(C, 4 * FP)
    rows = lax.all_gather(piece, ("y", "c"))

    def all_levels(start, tau, kernels, kernels_other, last, edges):
        other = swap(tau)
        levels, received, swapped = None, None, None
        packs = [jnp.zeros(PACK, BF16)] * 3
        for p in range(PLANES):
            if p == PLANES - 1 and edges is not None:
                mine, others, *packs = lax.optimization_barrier((*edges, *packs))
                swapped = swap(others)
                rows = jnp.where(c == 1, mine[BLOCKS - 1 :], swapped[BLOCKS - 1 :])
                received = lax.ppermute(rows, "x", [(q, q + 1) for q in range(PLANES - 1)])
            levels, pack = chain(
                p, edges is not None, place, packs, start, tau, other, kernels, kernels_other, levels
            )
            if p == 0 and edges is None:
                pack, last = lax.optimization_barrier((pack, last))
            if p + 1 < PLANES:
                packs = upward(pack, p)
            if p == 0 and edges is None:
                received = hand_over(last)
        return levels, swapped, received

    tau, ends, wk, ck, last, tile, start = first_sweeps(place, fetched, rows)
    ck_other = swap(ck)
    levels, _, received = all_levels(start, tau, ck, ck_other, last, None)

    before = ends.at[0].set(jnp.where((x == 0) & (c == 0), tile, received.reshape(TILE)))
    tau, edge, edge_other = later_sweeps(place, wk, ck, before, levels)
    levels, swapped, received = all_levels(start, tau, ck, ck_other, None, (edge, edge_other))

    parts = final(place, tile, edge, swapped, received, levels)
    got = lax.all_to_all(parts, "z", 0, 0, tiled=True)
    return got.reshape(ZS, C, 4, 2 * OWN).transpose(1, 2, 0, 3).reshape(1, C, 4, WIDTH)


def solution(mesh):
    split = Mesh(mesh.devices.reshape(PLANES, ZS, YS, 2), ("x", "z", "y", "c"))
    return jax.shard_map(
        per_device,
        mesh=split,
        in_specs=(P(None, ("y", "c"), None), P(("x", "z"), None, None)),
        out_specs=P(("x", "z"), None, ("y", "c"), None),
        check_vma=False,
    )
```

```python
import functools

import jax
import jax.numpy as jnp
from jax import lax
from jax.experimental import pallas as pl
from jax.experimental.pallas import tpu as pltpu
from jax.sharding import Mesh
from jax.sharding import PartitionSpec as P


STEP = 0.125
C = 64
FU, CU = 22, 11
HEIGHT = 64
FP, CP = 80, 40
FL, CL = 256, 128
OWN = 16
EDGE = 11
WIDTH = 256
BLOCKS = 4
PLANES, ZS, YS = 4, 8, 8
F32, BF16 = jnp.float32, jnp.bfloat16


def unit(u, count=1):
    start = u * C
    if not isinstance(u, int):
        start = pl.multiple_of(start, C)
    return pl.ds(start, count * C)


def lane_of(shape):
    return lax.broadcasted_iota(jnp.int32, shape, 1)


def pool_matrix():
    rows = lax.broadcasted_iota(jnp.int32, (FL, CL), 0)
    return jnp.where((rows >> 1) == lane_of((FL, CL)), 0.25, 0.0).astype(BF16)


def widen_matrix():
    rows = lax.broadcasted_iota(jnp.int32, (CL, FL), 0)
    return jnp.where(rows == (lane_of((CL, FL)) >> 1), 1.0, 0.0).astype(BF16)


def part_of(lane, pitch):
    return (lane >= pitch).astype(jnp.int32) + (lane >= 2 * pitch).astype(jnp.int32)


def within(lane, pitch):
    return lane - pitch * part_of(lane, pitch)


def factors(z, lanes, pitch, edge, own, width, value):
    lane = lane_of((1, lanes))
    column = within(lane, pitch) + (own * z - edge)
    inside = (column >= 0) & (column < width) & (lane < 3 * pitch)
    full = jnp.where(inside, value, 0.0).astype(F32)
    return full, jnp.where(lane < 2 * pitch, full, 0.0)


def fine_factors(z):
    return factors(z, FL, FP, 2 * EDGE, 2 * OWN, WIDTH, STEP)


def coarse_factors(z):
    return factors(z, CL, CP, EDGE, OWN, WIDTH // 2, BLOCKS * STEP)


def dot(a, b):
    return jnp.dot(a, b, preferred_element_type=F32)


def shifted_sum(product):
    lanes = product.shape[1]
    return pltpu.roll(product[:C], 1, 1) + product[C : 2 * C] + pltpu.roll(product[2 * C :], lanes - 1, 1)


def arranged(kernel):
    return jnp.concatenate(
        [
            jnp.concatenate(
                [kernel[:, (3 * dy + dx) * C : (3 * dy + dx + 1) * C] for dy in range(3)], axis=1
            )
            for dx in range(3)
        ],
        axis=0,
    )


def around(first, last, pitch):
    lanes = first.shape[1]
    lane = lane_of(first.shape)
    front = jnp.where((lane >= pitch) & (lane < 3 * pitch), pltpu.roll(last, pitch, 1), 0.0)
    behind = jnp.where(lane < 2 * pitch, pltpu.roll(first, lanes - pitch, 1), 0.0)
    return front.astype(BF16), behind.astype(BF16)


def fine_halo(ref):
    front, behind = around(ref[unit(1), :].astype(F32), ref[unit(FU), :].astype(F32), FP)
    ref[unit(0), :] = front
    ref[unit(FU + 1), :] = behind


def coarse_halo(ref, first, last):
    front, behind = around(first, last, CP)
    ref[unit(0), :] = front
    ref[unit(CU + 1), :] = behind


CHUNK = 4


def pooled_rows(rows, matrix):
    halves = dot(rows, matrix)
    return [
        halves[2 * i * C : (2 * i + 1) * C] + halves[(2 * i + 1) * C : (2 * i + 2) * C]
        for i in range(rows.shape[0] // (2 * C))
    ]


def corrected(first, second, level, pooled, widen):
    change = level - pooled
    high = change.astype(BF16)
    low = (change - high.astype(F32)).astype(BF16)
    wide = dot(high, widen) + dot(low, widen)
    return (first.astype(F32) + wide).astype(BF16), (second.astype(F32) + wide).astype(BF16)


def states_from_rows(xa, rows, level, pool, widen):
    for u in range(0, CU, CHUNK):
        count = min(CHUNK, CU - u)
        block = rows[0, 2 * u : 2 * u + 2 * count].reshape(2 * count * C, FL)
        for i, pooled in enumerate(pooled_rows(block, pool)):
            one, two = corrected(
                rows[0, 2 * (u + i)], rows[0, 2 * (u + i) + 1], level[0, u + i], pooled, widen
            )
            xa[unit(2 * (u + i) + 1), :] = one
            xa[unit(2 * (u + i) + 2), :] = two


def states_from_tile(xa, tile):
    for u in range(FU):
        xa[unit(u + 1), :] = tile[u]


def pool_states(xa, sp, sb, pool):
    for u in range(0, CU, CHUNK):
        count = min(CHUNK, CU - u)
        for i, s in enumerate(pooled_rows(xa[unit(2 * u + 1, 2 * count), :], pool)):
            sp[u + i] = s
            sb[unit(u + i + 1), :] = s.astype(BF16)
    coarse_halo(sb, sp[0], sp[CU - 1])


def run_layers(wk, xa, xb, mf):
    def layer(l, src, dst):
        kernel = wk[0, l]
        for u in range(FU):
            conv = shifted_sum(dot(kernel, src[unit(u, 3), :]))
            x = src[unit(u + 1), :].astype(F32)
            dst[unit(u + 1), :] = (x + mf[u >= FU - 2] * jnp.tanh(conv)).astype(BF16)
        fine_halo(dst)

    layer(0, xa, xb)
    layer(1, xb, xa)
    layer(2, xa, xb)
    layer(3, xb, xa)


def write_tau(ck, xa, sp, sb, tau_out, pool, mc):
    kernel = ck[0]
    for u in range(0, CU, CHUNK):
        count = min(CHUNK, CU - u)
        for i, ends in enumerate(pooled_rows(xa[unit(2 * u + 1, 2 * count), :], pool)):
            conv = shifted_sum(dot(kernel, sb[unit(u + i, 3), :]))
            tau_out[0, u + i] = (ends - (sp[u + i] + mc[u + i == CU - 1] * jnp.tanh(conv))).astype(BF16)


def first_kernel(sc, w0, w1, w2, w3, source, tau, ends, wk, ck, last, tile, sp, xa, xb, sb, sem):
    step = pl.program_id(0)
    z = sc[1]
    block = (z + step) & (BLOCKS - 1)
    pool = pool_matrix()

    def take(w):
        for l in range(4):
            wk[0, l] = arranged(w[l])
        total = w[0].astype(F32) + w[1].astype(F32) + w[2].astype(F32) + w[3].astype(F32)
        ck[0] = arranged((total * 0.25).astype(BF16))

    for i, w in enumerate((w0, w1, w2, w3)):
        pl.when(step == i)(functools.partial(take, w))

    @pl.when(step == 0)
    def _():
        zero = jnp.zeros((C, FP), BF16)

        def piece(row):
            if row >= HEIGHT:
                return zero
            strip, i = row // 4, row % 4
            return source[strip, :, i * FP : (i + 1) * FP]

        for u in range(FU):
            parts = [piece(u), piece(FU + u), piece(2 * FU + u), zero[:, : FL - 3 * FP]]
            tile[u] = jnp.concatenate(parts, axis=1)

    states_from_tile(xa, tile)
    fine_halo(xa)
    pl.when(step == 0)(lambda: pool_states(xa, sp, sb, pool))
    run_layers(wk, xa, xb, fine_factors(z))

    def to_last():
        return pltpu.make_async_copy(xa.at[pl.ds(C, FU * C), :], last, sem)

    pl.when(block == BLOCKS - 1)(lambda: to_last().start())
    for u in range(FU):
        ends[0, u] = xa[unit(u + 1), :]
    write_tau(ck, xa, sp, sb, tau, pool, coarse_factors(z))
    pl.when(block == BLOCKS - 1)(lambda: to_last().wait())


def later_kernel(sc, wk, ck, before, level, tau, edge, edge_other, xa, xb, sp, sb):
    z, y, c = sc[1], sc[2], sc[3]
    pool = pool_matrix()
    states_from_rows(xa, before, level, pool, widen_matrix())
    fine_halo(xa)
    pool_states(xa, sp, sb, pool)
    run_layers(wk, xa, xb, fine_factors(z))
    for out, k in ((edge, c), (edge_other, 1 - c)):
        for r in range(4):
            row = 8 * y + 4 * k + r
            out[0, r] = xa[unit(row - FU * part_of(row, FU) + 1), :]
    write_tau(ck, xa, sp, sb, tau, pool, coarse_factors(z))


def whole(shape):
    return pl.BlockSpec(shape, lambda i, s: (0,) * len(shape))


def at_step(shape):
    return pl.BlockSpec((1,) + shape, lambda i, s: (i,) + (0,) * len(shape))


def at_slot(shape, by=0):
    return pl.BlockSpec((1,) + shape, lambda i, s: (((s[1] + i) & (BLOCKS - 1)) + by,) + (0,) * len(shape))


ANY = pl.BlockSpec(memory_space=pl.ANY)
ROWS_AT = 16
TAU = (BLOCKS, CU, C, CL)
ENDS = (BLOCKS + 1, FU, C, FL)
EDGES = (BLOCKS, 4, C, FL)
ROWS = (2 * BLOCKS, 2, C, CL)
TILE = (FU, C, FL)
START = (CU, C, CL)
KERS = (BLOCKS, 4, 3 * C, 3 * C)
KER = (BLOCKS, 3 * C, 3 * C)
LAST = (FU * C, FL)
VMEM_LIMIT = 56 * 1024 * 1024
STATES = [
    pltpu.VMEM(((FU + 2) * C, FL), BF16),
    pltpu.VMEM(((FU + 2) * C, FL), BF16),
]
POOLED = [pltpu.VMEM(((CU + 2) * C, CL), BF16)]


def sweep_cost(count):
    return pl.CostEstimate(
        flops=2 * count * 4 * 192 * 192 * FU * FL,
        bytes_accessed=count * (4 << 20),
        transcendentals=count * 4 * C * FU * FL,
    )


def first_sweeps(place, weights, source):
    return pl.pallas_call(
        first_kernel,
        out_shape=[
            jax.ShapeDtypeStruct(TAU, BF16),
            jax.ShapeDtypeStruct(ENDS, BF16),
            jax.ShapeDtypeStruct(KERS, BF16),
            jax.ShapeDtypeStruct(KER, BF16),
            jax.ShapeDtypeStruct(LAST, BF16),
            jax.ShapeDtypeStruct(TILE, BF16),
            jax.ShapeDtypeStruct(START, F32),
        ],
        grid_spec=pltpu.PrefetchScalarGridSpec(
            num_scalar_prefetch=1,
            grid=(BLOCKS,),
            in_specs=[whole((4, C, 9 * C))] * 4 + [whole((ROWS_AT, C, 4 * FP))],
            out_specs=[
                at_slot(TAU[1:]),
                at_slot(ENDS[1:], 1),
                at_slot(KERS[1:]),
                at_slot(KER[1:]),
                ANY,
                whole(TILE),
                whole(START),
            ],
            scratch_shapes=STATES + POOLED + [pltpu.SemaphoreType.DMA],
        ),
        compiler_params=pltpu.CompilerParams(vmem_limit_bytes=VMEM_LIMIT),
        cost_estimate=sweep_cost(BLOCKS),
    )(place, *weights, source)


def later_sweeps(place, wk, ck, before, levels):
    return pl.pallas_call(
        later_kernel,
        out_shape=[
            jax.ShapeDtypeStruct(TAU, BF16),
            jax.ShapeDtypeStruct(EDGES, BF16),
            jax.ShapeDtypeStruct(EDGES, BF16),
        ],
        grid_spec=pltpu.PrefetchScalarGridSpec(
            num_scalar_prefetch=1,
            grid=(BLOCKS,),
            in_specs=[at_step(KERS[1:]), at_step(KER[1:]), at_step(ENDS[1:]), at_step(TAU[1:])],
            out_specs=[at_step(TAU[1:]), at_step(EDGES[1:]), at_step(EDGES[1:])],
            scratch_shapes=STATES + [pltpu.VMEM(START, F32)] + POOLED,
        ),
        compiler_params=pltpu.CompilerParams(vmem_limit_bytes=VMEM_LIMIT),
        cost_estimate=sweep_cost(BLOCKS),
    )(place, wk, ck, before, levels)


def chain_kernel(plane, ending, sc, below, same, above, start, tau_own, tau_other, ck_own, ck_other, *refs):
    opening = plane == 0
    if opening:
        levels, pack, lf, la, lb, ks, ts, lv, lr, pk, sems, out_sems = refs
    else:
        _, levels, pack, lf, la, lb, ks, ts, lv, lr, pk, sems, out_sems = refs
    x, z, y, c = sc[0], sc[1], sc[2], sc[3]

    def half(h):
        return slice(128 * h, 128 * h + 128)

    def fetches(j, tau, kernel):
        at = j & (BLOCKS - 1)
        return (
            pltpu.make_async_copy(kernel.at[at], ks.at[j], sems.at[2 * BLOCKS + j]),
            pltpu.make_async_copy(tau.at[at], ts.at[j], sems.at[j]),
        )

    def begin(j):
        def start(tau, kernel):
            for copy in fetches(j, tau, kernel):
                copy.start()

        pl.when((j >> 2) == c)(lambda: start(tau_own, ck_own))
        pl.when((j >> 2) != c)(lambda: start(tau_other, ck_other))

    def level_copy(slot):
        return pltpu.make_async_copy(lv.at[slot], levels.at[slot], out_sems.at[slot])

    @pl.when(x == plane)
    def _():
        if opening:
            begin_at = [pltpu.make_async_copy(start, lv.at[BLOCKS], sems.at[4 * BLOCKS])]
        else:
            begin_at = [
                pltpu.make_async_copy(ref, pk.at[i], sems.at[4 * BLOCKS + i])
                for i, ref in enumerate((below, same, above))
            ]
        for copy in begin_at:
            copy.start()
        for j in range(AHEAD):
            begin(j)
        mc = coarse_factors(z)
        lane = within(lane_of((C, CL)), CP)
        inside = lane_of((C, CL)) < 3 * CP
        for copy in begin_at:
            copy.wait()

        def halo_of(ref):
            front, behind = around(lf[unit(0), half(0)], lf[unit(4), half(1)], CP)
            ref[unit(0), half(0)] = front
            ref[unit(0), half(1)] = lf[unit(5), half(0)].astype(BF16)
            ref[unit(7), half(0)] = lf[unit(0), half(1)].astype(BF16)
            ref[unit(6), half(1)] = behind

        def put(u, h, value):
            lf[unit(u), half(h)] = value
            la[unit(u + 1), half(h)] = value.astype(BF16)

        if opening:
            lf[unit(HU - 1), half(1)] = jnp.zeros((C, CL), F32)

            @pl.loop(0, HU)
            def _(u):
                put(u, 0, lv[BLOCKS, u])

            @pl.loop(0, CU - HU)
            def _(u):
                put(u, 1, lv[BLOCKS, HU + u])

        else:

            @pl.loop(0, HU // 2)
            def _(a):
                for h in range(2):
                    pieces = [pk[n, a + h * (HU // 2)].astype(F32) for n in range(3)]
                    for i in range(2):

                        def placed(n, by):
                            return pltpu.roll(pieces[n], (by - 16 * i) % 128, 1)

                        value = jnp.where(lane < EDGE, placed(0, EDGE - 16), placed(1, EDGE))
                        value = jnp.where(lane < EDGE + OWN, value, placed(2, EDGE + 16))
                        put(2 * a + i, h, jnp.where((lane >= 2) & (lane < 36) & inside, value, 0.0))

        halo_of(la)

        def step(j, src, dst):
            own = (j >> 2) == c
            slot = jnp.where(own, j & (BLOCKS - 1), BLOCKS)
            pl.when(j + AHEAD < 2 * BLOCKS)(lambda: begin(j + AHEAD))
            for copy in fetches(j, tau_own, ck_own):
                copy.wait()
            kernel = ks[j]
            if ending:
                for r in range(2):
                    row = 4 * y + 2 * c + r
                    u = row - CU * part_of(row, CU)
                    h = (u >= HU).astype(jnp.int32)
                    rows = lf[unit(u - HU * h), :]
                    lr[j, r] = jnp.where(h == 1, rows[:, half(1)], rows[:, half(0)])
            for u in range(HU):
                product = dot(kernel, src[unit(u, 3), :])
                for h in range(2):
                    if u + HU * h >= CU:
                        continue
                    conv = shifted_sum(product[:, half(h)])
                    old = lf[unit(u), half(h)]
                    if not ending:
                        lv[slot, u + HU * h] = old
                    new = old + mc[u + HU * h == CU - 1] * jnp.tanh(conv) + ts[j, u + HU * h].astype(F32)
                    lf[unit(u), half(h)] = new
                    dst[unit(u + 1), half(h)] = new.astype(BF16)
            halo_of(dst)
            if not ending:
                pl.when(own)(lambda: level_copy(j & (BLOCKS - 1)).start())

        @pl.loop(0, BLOCKS)
        def _(t):
            step(2 * t, la, lb)
            step(2 * t + 1, lb, la)

        @pl.loop(0, HU // 2)
        def _(a):
            for h in range(2):
                total = jnp.zeros((C, CL), F32)
                for i in range(2):
                    moved = pltpu.roll(lf[unit(2 * a + i), half(h)], (16 * i - EDGE) % 128, 1)
                    total = jnp.where((lane >= 16 * i) & (lane < 16 * i + 16), moved, total)
                pk[0, a + h * (HU // 2)] = total.astype(BF16)

        out = pltpu.make_async_copy(pk.at[0], pack, sems.at[4 * BLOCKS])
        out.start()
        if ending:
            rows_out = pltpu.make_async_copy(lr, levels, out_sems.at[0])
            rows_out.start()
            rows_out.wait()
        else:
            for slot in range(BLOCKS):
                level_copy(slot).wait()
        out.wait()


PACK = (6, C, CL)
HU = 6
AHEAD = 3


def chain(plane, ending, place, packs, start, tau_own, tau_other, ck_own, ck_other, held=None):
    operands = [*packs, start, tau_own, tau_other, ck_own, ck_other] + ([] if plane == 0 else [held])
    return pl.pallas_call(
        functools.partial(chain_kernel, plane, ending),
        out_shape=[jax.ShapeDtypeStruct(ROWS if ending else TAU, F32), jax.ShapeDtypeStruct(PACK, BF16)],
        in_specs=[pl.BlockSpec(memory_space=pltpu.SMEM)] + [ANY] * len(operands),
        out_specs=[ANY, ANY],
        scratch_shapes=[
            pltpu.VMEM((HU * C, FL), F32),
            pltpu.VMEM(((HU + 2) * C, FL), BF16),
            pltpu.VMEM(((HU + 2) * C, FL), BF16),
            pltpu.VMEM((2 * BLOCKS, 3 * C, 3 * C), BF16),
            pltpu.VMEM((2 * BLOCKS, CU, C, CL), BF16),
            pltpu.VMEM((BLOCKS + 1, CU, C, CL), F32),
            pltpu.VMEM(ROWS, F32),
            pltpu.VMEM((3,) + PACK, BF16),
            pltpu.SemaphoreType.DMA((4 * BLOCKS + 3,)),
            pltpu.SemaphoreType.DMA((BLOCKS,)),
        ],
        input_output_aliases={} if plane == 0 else {9: 0},
        compiler_params=pltpu.CompilerParams(vmem_limit_bytes=VMEM_LIMIT),
        cost_estimate=pl.CostEstimate(
            flops=2 * 8 * 192 * 192 * CU * CL, bytes_accessed=6 << 20, transcendentals=8 * CU * C * CL
        ),
    )(place, *operands)


def final_kernel(sc, tile, edge, edge_swapped, recv, level, out):
    fresh, y, c = sc[0] == 0, sc[2], sc[3]
    pool, widen = pool_matrix(), widen_matrix()
    lane = lane_of((C, 128))

    def choose(here, a, b):
        return jnp.where(here, a.astype(F32), b.astype(F32)).astype(BF16)

    pairs = [4 * y + 2 * c + pair for pair in range(2)]
    parts = [part_of(pair, CU) for pair in pairs]
    firsts = [2 * (pair - CU * part) for pair, part in zip(pairs, parts)]
    for j in range(2 * BLOCKS):
        packed = jnp.zeros((C, 128), F32)
        for pair in range(2):
            first = firsts[pair]
            if j == 0:
                rows = [
                    choose(fresh, tile[first + r], recv[0, 2 * pair + r]) for r in range(2)
                ]
            else:
                h, i = (j - 1) // BLOCKS, (j - 1) % BLOCKS
                rows = [
                    choose(c == h, edge[i, 2 * pair + r], edge_swapped[i, 2 * pair + r]) for r in range(2)
                ]
            pooled = dot(rows[0], pool) + dot(rows[1], pool)
            if j == 0:
                goal = jnp.where(fresh, pooled, level[0, pair])
            else:
                goal = level[j, pair]
            for r, row in enumerate(corrected(rows[0], rows[1], goal, pooled, widen)):
                row = row.astype(F32)
                i = 2 * pair + r
                moved = pltpu.roll(row, (FL - 2 * EDGE + 32 * i - FP * parts[pair]) & (FL - 1), 1)[:, :128]
                packed = jnp.where((lane >= 32 * i) & (lane < 32 * i + 32), moved, packed)
        out[j] = packed.astype(BF16)


def final(place, tile, edge, edge_swapped, received, rows):
    return pl.pallas_call(
        final_kernel,
        out_shape=jax.ShapeDtypeStruct((2 * BLOCKS, C, 128), BF16),
        grid_spec=pltpu.PrefetchScalarGridSpec(
            num_scalar_prefetch=1,
            grid=(1,),
            in_specs=[
                whole(TILE),
                whole(EDGES),
                whole(EDGES),
                whole((1,) + EDGES[1:]),
                whole(ROWS),
            ],
            out_specs=whole((2 * BLOCKS, C, 128)),
        ),
        compiler_params=pltpu.CompilerParams(vmem_limit_bytes=VMEM_LIMIT),
    )(place, tile, edge, edge_swapped, received, rows)


def kernel_sources(i):
    pairs = []
    for z in range(ZS):
        for c in range(2):
            source = 4 * c + (z + i) % 4
            pairs.append((source * 2 + z // 4, z * 2 + c))
    return pairs


def per_device(image, weights):
    x, z, y, c = (lax.axis_index(name) for name in ("x", "z", "y", "c"))
    place = jnp.stack([x, z, y, c]).astype(jnp.int32)

    def swap(a):
        return lax.ppermute(a, "c", [(0, 1), (1, 0)])

    def hand_over(last):
        pairs = []
        for p in range(PLANES):
            pairs.append((2 * p, 2 * p + 1))
            if p + 1 < PLANES:
                pairs.append((2 * p + 1, 2 * p + 2))
        return lax.ppermute(last, ("x", "c"), pairs)

    def upward(pack, p):
        got = []
        for shift in (1, 0, -1):
            pairs = [
                (p * ZS + q, (p + 1) * ZS + q + shift) for q in range(ZS) if 0 <= q + shift < ZS
            ]
            got.append(lax.ppermute(pack, ("x", "z"), pairs))
        return got

    fetched = [lax.ppermute(weights, ("z", "c"), kernel_sources(i)) for i in range(BLOCKS)]
    wide = jnp.pad(image, ((0, 0), (0, 0), (2 * EDGE, 128)))
    piece = lax.dynamic_slice_in_dim(wide, 2 * OWN * z, FP, axis=2).reshape(C, 4 * FP)
    rows = lax.all_gather(piece, ("y", "c"))

    def all_levels(start, tau, kernels, kernels_other, last, edges):
        other = swap(tau)
        levels, swapped = None, None
        received = hand_over(last) if edges is None else None
        packs = [jnp.zeros(PACK, BF16)] * 3
        for p in range(PLANES):
            if p == PLANES - 1 and edges is not None:
                mine, others, *packs = lax.optimization_barrier((*edges, *packs))
                swapped = swap(others)
                rows = jnp.where(c == 1, mine[BLOCKS - 1 :], swapped[BLOCKS - 1 :])
                received = lax.ppermute(rows, "x", [(q, q + 1) for q in range(PLANES - 1)])
            levels, pack = chain(
                p, edges is not None, place, packs, start, tau, other, kernels, kernels_other, levels
            )
            if p + 1 < PLANES:
                packs = upward(pack, p)
        return levels, swapped, received

    tau, ends, wk, ck, last, tile, start = first_sweeps(place, fetched, rows)
    ck_other = swap(ck)
    levels, _, received = all_levels(start, tau, ck, ck_other, last, None)

    before = ends.at[0].set(jnp.where((x == 0) & (c == 0), tile, received.reshape(TILE)))
    tau, edge, edge_other = later_sweeps(place, wk, ck, before, levels)
    levels, swapped, received = all_levels(start, tau, ck, ck_other, None, (edge, edge_other))

    parts = final(place, tile, edge, swapped, received, levels)
    got = lax.all_to_all(parts, "z", 0, 0, tiled=True)
    return got.reshape(ZS, C, 4, 2 * OWN).transpose(1, 2, 0, 3).reshape(1, C, 4, WIDTH)


def solution(mesh):
    split = Mesh(mesh.devices.reshape(PLANES, ZS, YS, 2), ("x", "z", "y", "c"))
    return jax.shard_map(
        per_device,
        mesh=split,
        in_specs=(P(None, ("y", "c"), None), P(("x", "z"), None, None)),
        out_specs=P(("x", "z"), None, ("y", "c"), None),
        check_vma=False,
    )
```

```python
import functools

import jax
import jax.numpy as jnp
from jax import lax
from jax.experimental import pallas as pl
from jax.experimental.pallas import tpu as pltpu
from jax.sharding import Mesh
from jax.sharding import PartitionSpec as P


STEP = 0.125
C = 64
FU, CU = 22, 11
HEIGHT = 64
FP, CP = 80, 40
FL, CL = 256, 128
OWN = 16
EDGE = 11
WIDTH = 256
BLOCKS = 4
PLANES, ZS, YS = 4, 8, 8
F32, BF16 = jnp.float32, jnp.bfloat16


def unit(u, count=1):
    start = u * C
    if not isinstance(u, int):
        start = pl.multiple_of(start, C)
    return pl.ds(start, count * C)


def lane_of(shape):
    return lax.broadcasted_iota(jnp.int32, shape, 1)


def pool_matrix():
    rows = lax.broadcasted_iota(jnp.int32, (FL, CL), 0)
    return jnp.where((rows >> 1) == lane_of((FL, CL)), 0.25, 0.0).astype(BF16)


def widen_matrix():
    rows = lax.broadcasted_iota(jnp.int32, (CL, FL), 0)
    return jnp.where(rows == (lane_of((CL, FL)) >> 1), 1.0, 0.0).astype(BF16)


def part_of(lane, pitch):
    return (lane >= pitch).astype(jnp.int32) + (lane >= 2 * pitch).astype(jnp.int32)


def within(lane, pitch):
    return lane - pitch * part_of(lane, pitch)


def factors(z, lanes, pitch, edge, own, width, value):
    lane = lane_of((1, lanes))
    column = within(lane, pitch) + (own * z - edge)
    inside = (column >= 0) & (column < width) & (lane < 3 * pitch)
    full = jnp.where(inside, value, 0.0).astype(F32)
    return full, jnp.where(lane < 2 * pitch, full, 0.0)


def fine_factors(z):
    return factors(z, FL, FP, 2 * EDGE, 2 * OWN, WIDTH, STEP)


def coarse_factors(z):
    return factors(z, CL, CP, EDGE, OWN, WIDTH // 2, BLOCKS * STEP)


def dot(a, b):
    return jnp.dot(a, b, preferred_element_type=F32)


def shifted_sum(product):
    lanes = product.shape[1]
    return pltpu.roll(product[:C], 1, 1) + product[C : 2 * C] + pltpu.roll(product[2 * C :], lanes - 1, 1)


def arranged(kernel):
    return jnp.concatenate(
        [
            jnp.concatenate(
                [kernel[:, (3 * dy + dx) * C : (3 * dy + dx + 1) * C] for dy in range(3)], axis=1
            )
            for dx in range(3)
        ],
        axis=0,
    )


def around(first, last, pitch):
    lanes = first.shape[1]
    lane = lane_of(first.shape)
    front = jnp.where((lane >= pitch) & (lane < 3 * pitch), pltpu.roll(last, pitch, 1), 0.0)
    behind = jnp.where(lane < 2 * pitch, pltpu.roll(first, lanes - pitch, 1), 0.0)
    return front.astype(BF16), behind.astype(BF16)


def fine_halo(ref):
    front, behind = around(ref[unit(1), :].astype(F32), ref[unit(FU), :].astype(F32), FP)
    ref[unit(0), :] = front
    ref[unit(FU + 1), :] = behind


def coarse_halo(ref, first, last):
    front, behind = around(first, last, CP)
    ref[unit(0), :] = front
    ref[unit(CU + 1), :] = behind


CHUNK = 4


def pooled_rows(rows, matrix):
    halves = dot(rows, matrix)
    return [
        halves[2 * i * C : (2 * i + 1) * C] + halves[(2 * i + 1) * C : (2 * i + 2) * C]
        for i in range(rows.shape[0] // (2 * C))
    ]


def corrected(first, second, level, pooled, widen):
    change = level - pooled
    high = change.astype(BF16)
    low = (change - high.astype(F32)).astype(BF16)
    wide = dot(high, widen) + dot(low, widen)
    return (first.astype(F32) + wide).astype(BF16), (second.astype(F32) + wide).astype(BF16)


def states_from_rows(xa, rows, level, pool, widen):
    for u in range(0, CU, CHUNK):
        count = min(CHUNK, CU - u)
        block = rows[0, 2 * u : 2 * u + 2 * count].reshape(2 * count * C, FL)
        for i, pooled in enumerate(pooled_rows(block, pool)):
            one, two = corrected(
                rows[0, 2 * (u + i)], rows[0, 2 * (u + i) + 1], level[0, u + i], pooled, widen
            )
            xa[unit(2 * (u + i) + 1), :] = one
            xa[unit(2 * (u + i) + 2), :] = two


def states_from_tile(xa, tile):
    for u in range(FU):
        xa[unit(u + 1), :] = tile[u]


def pool_states(xa, sp, sb, pool):
    for u in range(0, CU, CHUNK):
        count = min(CHUNK, CU - u)
        for i, s in enumerate(pooled_rows(xa[unit(2 * u + 1, 2 * count), :], pool)):
            sp[u + i] = s
            sb[unit(u + i + 1), :] = s.astype(BF16)
    coarse_halo(sb, sp[0], sp[CU - 1])


def run_layers(wk, xa, xb, mf):
    def layer(l, src, dst):
        kernel = wk[0, l]
        for u in range(FU):
            conv = shifted_sum(dot(kernel, src[unit(u, 3), :]))
            x = src[unit(u + 1), :].astype(F32)
            dst[unit(u + 1), :] = (x + mf[u >= FU - 2] * jnp.tanh(conv)).astype(BF16)
        fine_halo(dst)

    layer(0, xa, xb)
    layer(1, xb, xa)
    layer(2, xa, xb)
    layer(3, xb, xa)


def write_tau(ck, xa, sp, sb, tau_out, pool, mc):
    kernel = ck[0]
    for u in range(0, CU, CHUNK):
        count = min(CHUNK, CU - u)
        for i, ends in enumerate(pooled_rows(xa[unit(2 * u + 1, 2 * count), :], pool)):
            conv = shifted_sum(dot(kernel, sb[unit(u + i, 3), :]))
            tau_out[0, u + i] = (ends - (sp[u + i] + mc[u + i == CU - 1] * jnp.tanh(conv))).astype(BF16)


def first_kernel(sc, w0, w1, w2, w3, source, tau, ends, wk, ck, last, tile, sp, xa, xb, sb, sem):
    step = pl.program_id(0)
    z = sc[1]
    block = (z + step) & (BLOCKS - 1)
    pool = pool_matrix()

    def take(w):
        for l in range(4):
            wk[0, l] = arranged(w[l])
        total = w[0].astype(F32) + w[1].astype(F32) + w[2].astype(F32) + w[3].astype(F32)
        ck[0] = arranged((total * 0.25).astype(BF16))

    for i, w in enumerate((w0, w1, w2, w3)):
        pl.when(step == i)(functools.partial(take, w))

    @pl.when(step == 0)
    def _():
        zero = jnp.zeros((C, FP), BF16)

        def piece(row):
            if row >= HEIGHT:
                return zero
            strip, i = row // 4, row % 4
            return source[strip, :, i * FP : (i + 1) * FP]

        for u in range(FU):
            parts = [piece(u), piece(FU + u), piece(2 * FU + u), zero[:, : FL - 3 * FP]]
            tile[u] = jnp.concatenate(parts, axis=1)

    states_from_tile(xa, tile)
    fine_halo(xa)
    pl.when(step == 0)(lambda: pool_states(xa, sp, sb, pool))
    run_layers(wk, xa, xb, fine_factors(z))

    def to_last():
        return pltpu.make_async_copy(xa.at[pl.ds(C, FU * C), :], last, sem)

    pl.when(block == BLOCKS - 1)(lambda: to_last().start())
    for u in range(FU):
        ends[0, u] = xa[unit(u + 1), :]
    write_tau(ck, xa, sp, sb, tau, pool, coarse_factors(z))
    pl.when(block == BLOCKS - 1)(lambda: to_last().wait())


def later_kernel(sc, wk, ck, before, level, tau, edge, edge_other, xa, xb, sp, sb):
    z, y, c = sc[1], sc[2], sc[3]
    pool = pool_matrix()
    states_from_rows(xa, before, level, pool, widen_matrix())
    fine_halo(xa)
    pool_states(xa, sp, sb, pool)
    run_layers(wk, xa, xb, fine_factors(z))
    for out, k in ((edge, c), (edge_other, 1 - c)):
        for r in range(4):
            row = 8 * y + 4 * k + r
            out[0, r] = xa[unit(row - FU * part_of(row, FU) + 1), :]
    write_tau(ck, xa, sp, sb, tau, pool, coarse_factors(z))


def whole(shape):
    return pl.BlockSpec(shape, lambda i, s: (0,) * len(shape))


def at_step(shape):
    return pl.BlockSpec((1,) + shape, lambda i, s: (i,) + (0,) * len(shape))


def at_slot(shape, by=0):
    return pl.BlockSpec((1,) + shape, lambda i, s: (((s[1] + i) & (BLOCKS - 1)) + by,) + (0,) * len(shape))


ANY = pl.BlockSpec(memory_space=pl.ANY)
ROWS_AT = 16
TAU = (BLOCKS, CU, C, CL)
ENDS = (BLOCKS + 1, FU, C, FL)
EDGES = (BLOCKS, 4, C, FL)
ROWS = (2 * BLOCKS, 2, C, CL)
TILE = (FU, C, FL)
START = (CU, C, CL)
KERS = (BLOCKS, 4, 3 * C, 3 * C)
KER = (BLOCKS, 3 * C, 3 * C)
LAST = (FU * C, FL)
VMEM_LIMIT = 56 * 1024 * 1024
STATES = [
    pltpu.VMEM(((FU + 2) * C, FL), BF16),
    pltpu.VMEM(((FU + 2) * C, FL), BF16),
]
POOLED = [pltpu.VMEM(((CU + 2) * C, CL), BF16)]


def sweep_cost(count):
    return pl.CostEstimate(
        flops=2 * count * 4 * 192 * 192 * FU * FL,
        bytes_accessed=count * (4 << 20),
        transcendentals=count * 4 * C * FU * FL,
    )


def first_sweeps(place, weights, source):
    return pl.pallas_call(
        first_kernel,
        out_shape=[
            jax.ShapeDtypeStruct(TAU, BF16),
            jax.ShapeDtypeStruct(ENDS, BF16),
            jax.ShapeDtypeStruct(KERS, BF16),
            jax.ShapeDtypeStruct(KER, BF16),
            jax.ShapeDtypeStruct(LAST, BF16),
            jax.ShapeDtypeStruct(TILE, BF16),
            jax.ShapeDtypeStruct(START, F32),
        ],
        grid_spec=pltpu.PrefetchScalarGridSpec(
            num_scalar_prefetch=1,
            grid=(BLOCKS,),
            in_specs=[whole((4, C, 9 * C))] * 4 + [whole((ROWS_AT, C, 4 * FP))],
            out_specs=[
                at_slot(TAU[1:]),
                at_slot(ENDS[1:], 1),
                at_slot(KERS[1:]),
                at_slot(KER[1:]),
                ANY,
                whole(TILE),
                whole(START),
            ],
            scratch_shapes=STATES + POOLED + [pltpu.SemaphoreType.DMA],
        ),
        compiler_params=pltpu.CompilerParams(vmem_limit_bytes=VMEM_LIMIT),
        cost_estimate=sweep_cost(BLOCKS),
    )(place, *weights, source)


def later_sweeps(place, wk, ck, before, levels):
    return pl.pallas_call(
        later_kernel,
        out_shape=[
            jax.ShapeDtypeStruct(TAU, BF16),
            jax.ShapeDtypeStruct(EDGES, BF16),
            jax.ShapeDtypeStruct(EDGES, BF16),
        ],
        grid_spec=pltpu.PrefetchScalarGridSpec(
            num_scalar_prefetch=1,
            grid=(BLOCKS,),
            in_specs=[at_step(KERS[1:]), at_step(KER[1:]), at_step(ENDS[1:]), at_step(TAU[1:])],
            out_specs=[at_step(TAU[1:]), at_step(EDGES[1:]), at_step(EDGES[1:])],
            scratch_shapes=STATES + [pltpu.VMEM(START, F32)] + POOLED,
        ),
        compiler_params=pltpu.CompilerParams(vmem_limit_bytes=VMEM_LIMIT),
        cost_estimate=sweep_cost(BLOCKS),
    )(place, wk, ck, before, levels)


def chain_kernel(plane, ending, sc, below, same, above, start, tau_own, tau_other, ck_own, ck_other, *refs):
    opening = plane == 0
    if opening:
        levels, pack, lf, la, lb, ks, ts, lv, lr, pk, sems, out_sems = refs
    else:
        _, levels, pack, lf, la, lb, ks, ts, lv, lr, pk, sems, out_sems = refs
    x, z, y, c = sc[0], sc[1], sc[2], sc[3]

    def half(h):
        return slice(128 * h, 128 * h + 128)

    def fetches(j, tau, kernel):
        at = j & (BLOCKS - 1)
        return (
            pltpu.make_async_copy(kernel.at[at], ks.at[j], sems.at[2 * BLOCKS + j]),
            pltpu.make_async_copy(tau.at[at], ts.at[j], sems.at[j]),
        )

    def begin(j):
        def start(tau, kernel):
            for copy in fetches(j, tau, kernel):
                copy.start()

        pl.when((j >> 2) == c)(lambda: start(tau_own, ck_own))
        pl.when((j >> 2) != c)(lambda: start(tau_other, ck_other))

    def level_copy(slot):
        return pltpu.make_async_copy(lv.at[slot], levels.at[slot], out_sems.at[slot])

    @pl.when(x == plane)
    def _():
        if opening:
            begin_at = [pltpu.make_async_copy(start, lv.at[BLOCKS], sems.at[4 * BLOCKS])]
        else:
            begin_at = [
                pltpu.make_async_copy(ref, pk.at[i], sems.at[4 * BLOCKS + i])
                for i, ref in enumerate((below, same, above))
            ]
        for copy in begin_at:
            copy.start()
        for j in range(AHEAD):
            begin(j)
        mc = coarse_factors(z)
        lane = within(lane_of((C, CL)), CP)
        inside = lane_of((C, CL)) < 3 * CP
        for copy in begin_at:
            copy.wait()

        def halo_of(ref):
            front, behind = around(lf[unit(0), half(0)], lf[unit(4), half(1)], CP)
            ref[unit(0), half(0)] = front
            ref[unit(0), half(1)] = lf[unit(5), half(0)].astype(BF16)
            ref[unit(7), half(0)] = lf[unit(0), half(1)].astype(BF16)
            ref[unit(6), half(1)] = behind

        def put(u, h, value):
            lf[unit(u), half(h)] = value
            la[unit(u + 1), half(h)] = value.astype(BF16)

        if opening:
            lf[unit(HU - 1), half(1)] = jnp.zeros((C, CL), F32)

            @pl.loop(0, HU)
            def _(u):
                put(u, 0, lv[BLOCKS, u])

            @pl.loop(0, CU - HU)
            def _(u):
                put(u, 1, lv[BLOCKS, HU + u])

        else:

            @pl.loop(0, HU // 2)
            def _(a):
                for h in range(2):
                    pieces = [pk[n, a + h * (HU // 2)].astype(F32) for n in range(3)]
                    for i in range(2):

                        def placed(n, by):
                            return pltpu.roll(pieces[n], (by - 16 * i) % 128, 1)

                        value = jnp.where(lane < EDGE, placed(0, EDGE - 16), placed(1, EDGE))
                        value = jnp.where(lane < EDGE + OWN, value, placed(2, EDGE + 16))
                        put(2 * a + i, h, jnp.where((lane >= 2) & (lane < 36) & inside, value, 0.0))

        halo_of(la)

        def step(j, src, dst):
            own = (j >> 2) == c
            slot = jnp.where(own, j & (BLOCKS - 1), BLOCKS)
            pl.when(j + AHEAD < 2 * BLOCKS)(lambda: begin(j + AHEAD))
            for copy in fetches(j, tau_own, ck_own):
                copy.wait()
            kernel = ks[j]
            if ending:
                for r in range(2):
                    row = 4 * y + 2 * c + r
                    u = row - CU * part_of(row, CU)
                    h = (u >= HU).astype(jnp.int32)
                    rows = lf[unit(u - HU * h), :]
                    lr[j, r] = jnp.where(h == 1, rows[:, half(1)], rows[:, half(0)])
            for u in range(HU):
                product = dot(kernel, src[unit(u, 3), :])
                for h in range(2):
                    if u + HU * h >= CU:
                        continue
                    conv = shifted_sum(product[:, half(h)])
                    old = lf[unit(u), half(h)]
                    if not ending:
                        lv[slot, u + HU * h] = old
                    new = old + mc[u + HU * h == CU - 1] * jnp.tanh(conv) + ts[j, u + HU * h].astype(F32)
                    lf[unit(u), half(h)] = new
                    dst[unit(u + 1), half(h)] = new.astype(BF16)
            halo_of(dst)
            if not ending:
                pl.when(own)(lambda: level_copy(j & (BLOCKS - 1)).start())

        @pl.loop(0, BLOCKS)
        def _(t):
            step(2 * t, la, lb)
            step(2 * t + 1, lb, la)

        @pl.loop(0, HU // 2)
        def _(a):
            for h in range(2):
                total = jnp.zeros((C, CL), F32)
                for i in range(2):
                    moved = pltpu.roll(lf[unit(2 * a + i), half(h)], (16 * i - EDGE) % 128, 1)
                    total = jnp.where((lane >= 16 * i) & (lane < 16 * i + 16), moved, total)
                pk[0, a + h * (HU // 2)] = total.astype(BF16)

        out = pltpu.make_async_copy(pk.at[0], pack, sems.at[4 * BLOCKS])
        out.start()
        if ending:
            rows_out = pltpu.make_async_copy(lr, levels, out_sems.at[0])
            rows_out.start()
            rows_out.wait()
        else:
            for slot in range(BLOCKS):
                level_copy(slot).wait()
        out.wait()


PACK = (6, C, CL)
HU = 6
AHEAD = 3


def chain(plane, ending, place, packs, start, tau_own, tau_other, ck_own, ck_other, held=None):
    operands = [*packs, start, tau_own, tau_other, ck_own, ck_other] + ([] if plane == 0 else [held])
    return pl.pallas_call(
        functools.partial(chain_kernel, plane, ending),
        out_shape=[jax.ShapeDtypeStruct(ROWS if ending else TAU, F32), jax.ShapeDtypeStruct(PACK, BF16)],
        in_specs=[pl.BlockSpec(memory_space=pltpu.SMEM)] + [ANY] * len(operands),
        out_specs=[ANY, ANY],
        scratch_shapes=[
            pltpu.VMEM((HU * C, FL), F32),
            pltpu.VMEM(((HU + 2) * C, FL), BF16),
            pltpu.VMEM(((HU + 2) * C, FL), BF16),
            pltpu.VMEM((2 * BLOCKS, 3 * C, 3 * C), BF16),
            pltpu.VMEM((2 * BLOCKS, CU, C, CL), BF16),
            pltpu.VMEM((BLOCKS + 1, CU, C, CL), F32),
            pltpu.VMEM(ROWS, F32),
            pltpu.VMEM((3,) + PACK, BF16),
            pltpu.SemaphoreType.DMA((4 * BLOCKS + 3,)),
            pltpu.SemaphoreType.DMA((BLOCKS,)),
        ],
        input_output_aliases={} if plane == 0 else {9: 0},
        compiler_params=pltpu.CompilerParams(vmem_limit_bytes=VMEM_LIMIT),
        cost_estimate=pl.CostEstimate(
            flops=2 * 8 * 192 * 192 * CU * CL, bytes_accessed=6 << 20, transcendentals=8 * CU * C * CL
        ),
    )(place, *operands)


def final_kernel(sc, tile, edge, edge_swapped, recv, level, out):
    fresh, y, c = sc[0] == 0, sc[2], sc[3]
    pool, widen = pool_matrix(), widen_matrix()
    lane = lane_of((C, 128))

    def choose(here, a, b):
        return jnp.where(here, a.astype(F32), b.astype(F32)).astype(BF16)

    pairs = [4 * y + 2 * c + pair for pair in range(2)]
    parts = [part_of(pair, CU) for pair in pairs]
    firsts = [2 * (pair - CU * part) for pair, part in zip(pairs, parts)]
    for j in range(2 * BLOCKS):
        packed = jnp.zeros((C, 128), F32)
        for pair in range(2):
            first = firsts[pair]
            if j == 0:
                rows = [
                    choose(fresh, tile[first + r], recv[0, 2 * pair + r]) for r in range(2)
                ]
            else:
                h, i = (j - 1) // BLOCKS, (j - 1) % BLOCKS
                rows = [
                    choose(c == h, edge[i, 2 * pair + r], edge_swapped[i, 2 * pair + r]) for r in range(2)
                ]
            pooled = dot(rows[0], pool) + dot(rows[1], pool)
            if j == 0:
                goal = jnp.where(fresh, pooled, level[0, pair])
            else:
                goal = level[j, pair]
            for r, row in enumerate(corrected(rows[0], rows[1], goal, pooled, widen)):
                row = row.astype(F32)
                i = 2 * pair + r
                moved = pltpu.roll(row, (FL - 2 * EDGE + 32 * i - FP * parts[pair]) & (FL - 1), 1)[:, :128]
                packed = jnp.where((lane >= 32 * i) & (lane < 32 * i + 32), moved, packed)
        out[j] = packed.astype(BF16)


def final(place, tile, edge, edge_swapped, received, rows):
    return pl.pallas_call(
        final_kernel,
        out_shape=jax.ShapeDtypeStruct((2 * BLOCKS, C, 128), BF16),
        grid_spec=pltpu.PrefetchScalarGridSpec(
            num_scalar_prefetch=1,
            grid=(1,),
            in_specs=[
                whole(TILE),
                whole(EDGES),
                whole(EDGES),
                whole((1,) + EDGES[1:]),
                whole(ROWS),
            ],
            out_specs=whole((2 * BLOCKS, C, 128)),
        ),
        compiler_params=pltpu.CompilerParams(vmem_limit_bytes=VMEM_LIMIT),
    )(place, tile, edge, edge_swapped, received, rows)


def kernel_sources(i):
    pairs = []
    for z in range(ZS):
        for c in range(2):
            source = 4 * c + (z + i) % 4
            pairs.append((source * 2 + z // 4, z * 2 + c))
    return pairs


def per_device(image, weights):
    x, z, y, c = (lax.axis_index(name) for name in ("x", "z", "y", "c"))
    place = jnp.stack([x, z, y, c]).astype(jnp.int32)

    def swap(a):
        return lax.ppermute(a, "c", [(0, 1), (1, 0)])

    def hand_over(last):
        pairs = []
        for p in range(PLANES):
            pairs.append((2 * p, 2 * p + 1))
            if p + 1 < PLANES:
                pairs.append((2 * p + 1, 2 * p + 2))
        return lax.ppermute(last, ("x", "c"), pairs)

    def upward(pack, p):
        got = []
        for shift in (1, 0, -1):
            pairs = [
                (p * ZS + q, (p + 1) * ZS + q + shift) for q in range(ZS) if 0 <= q + shift < ZS
            ]
            got.append(lax.ppermute(pack, ("x", "z"), pairs))
        return got

    fetched = [lax.ppermute(weights, ("z", "c"), kernel_sources(i)) for i in range(BLOCKS)]
    wide = jnp.pad(image, ((0, 0), (0, 0), (2 * EDGE, 128)))
    piece = lax.dynamic_slice_in_dim(wide, 2 * OWN * z, FP, axis=2).reshape(C, 4 * FP)
    rows = lax.all_gather(piece, ("y", "c"))

    def all_levels(start, tau, kernels, kernels_other, last, edges):
        other = swap(tau)
        levels, swapped = None, None
        received = hand_over(last) if edges is None else None
        packs = [jnp.zeros(PACK, BF16)] * 3
        for p in range(PLANES):
            levels, pack = chain(
                p, edges is not None, place, packs, start, tau, other, kernels, kernels_other, levels
            )
            late = p == PLANES - 2 and edges is not None
            if late:
                mine, others, pack = lax.optimization_barrier((*edges, pack))
            if p + 1 < PLANES:
                packs = upward(pack, p)
            if late:
                swapped = swap(others)
                rows = jnp.where(c == 1, mine[BLOCKS - 1 :], swapped[BLOCKS - 1 :])
                received = lax.ppermute(rows, "x", [(q, q + 1) for q in range(PLANES - 1)])
        return levels, swapped, received

    tau, ends, wk, ck, last, tile, start = first_sweeps(place, fetched, rows)
    ck_other = swap(ck)
    levels, _, received = all_levels(start, tau, ck, ck_other, last, None)

    before = ends.at[0].set(jnp.where((x == 0) & (c == 0), tile, received.reshape(TILE)))
    tau, edge, edge_other = later_sweeps(place, wk, ck, before, levels)
    levels, swapped, received = all_levels(start, tau, ck, ck_other, None, (edge, edge_other))

    parts = final(place, tile, edge, swapped, received, levels)
    got = lax.all_to_all(parts, "z", 0, 0, tiled=True)
    return got.reshape(ZS, C, 4, 2 * OWN).transpose(1, 2, 0, 3).reshape(1, C, 4, WIDTH)


def solution(mesh):
    split = Mesh(mesh.devices.reshape(PLANES, ZS, YS, 2), ("x", "z", "y", "c"))
    return jax.shard_map(
        per_device,
        mesh=split,
        in_specs=(P(None, ("y", "c"), None), P(("x", "z"), None, None)),
        out_specs=P(("x", "z"), None, ("y", "c"), None),
        check_vma=False,
    )
```
